32 devices in a mesh: row: 4 (over x, core), col: 8 (over z, y).
Axes of the slice: x: 2, y: 2, z: 4, core: 2. Of those that a mesh axis runs over, the one named last changes fastest.
Arguments:
- samples: float32 [384, 8192], P(None, ('row', 'col')), may hold values from -6 to 6
- omega_tiles: float32 [4, 8, 15, 256, 256], P('row', 'col'), may hold values from -6 to 6
- omega_diag: float32 [8192, 256], P(('row', 'col')), as said below
- tile_rows: int32 [4, 8, 15], P('row', 'col'), may hold values from 0 to 7, as said below
- tile_cols: int32 [4, 8, 15], P('row', 'col'), may hold values from 0 to 3
- tile_active: int32 [4, 8, 15], P('row', 'col'), may hold values from 0 to 1, as said below
Outputs:
- new_tiles: float32 [4, 8, 15, 256, 256], P('row', 'col')
- new_diag: float32 [8192, 256], P(('row', 'col'))
The draws below stay inside these ranges and needn't reach their ends.
Inputs may be any that keep to these rules, and one draw needn't show every extreme that they name: `tile_rows`: on each device the 15 listed tiles (I, J) are distinct and none is diagonal; with o = (J - I) mod (32), o is odd and below 16, or even and above it, so no tile is listed together with its mirror. `tile_active`: on each device the live slots come first and number at least 5; on device (0, 0) all are live. `omega_diag`: every diagonal tile is symmetric and its diagonal entries lie between 0.5 and 4.
All inputs are finite; a program needn't handle non-finite values.
Results may differ from the reference program's by a relative error of at most 0.0003.
Values sent between devices are 32-bit elements; how exact they have to be, the bound alone decides.
No kernel may reach another device: no remote copies, remote signals or barrier semaphores. Data moves between devices by JAX's collectives and lax.ppermute only.
A program may use at most 128 MiB of HBM per device.

```python
import jax
import jax.numpy as jnp
from jax import lax

B = 256
NSAMP = 384
SLOTS = 15
P_SIZE = 8192
N_ROW = 4
N_COL = 8


def support_pair(key):
    device_count = N_ROW * N_COL
    half_count = device_count // 2
    offsets_all = jnp.arange(1, device_count, dtype=jnp.int32)
    odd_flag = offsets_all % 2
    valid = (odd_flag == 1) & (offsets_all < half_count) | (odd_flag == 0) & (offsets_all > half_count)

    def per_device(device):
        row_index = device // N_COL
        col_index = device % N_COL
        ranks = jax.random.permutation(jax.random.fold_in(key, device), device_count - 1).astype(jnp.int32)
        scores = jnp.where(valid, ranks, ranks + device_count)
        order = jnp.argsort(scores, stable=True).astype(jnp.int32)
        offsets = offsets_all[order[:SLOTS]]
        block_row = (col_index - offsets) % N_COL
        steps_up = (offsets - (col_index - block_row)) % device_count // N_COL
        block_col = (row_index + steps_up) % N_ROW
        return (block_row.astype(jnp.int32), block_col.astype(jnp.int32))
    rows_all, cols_all = jax.vmap(per_device)(jnp.arange(device_count, dtype=jnp.int32))
    return (rows_all.reshape(N_ROW, N_COL, SLOTS), cols_all.reshape(N_ROW, N_COL, SLOTS))


def draw_tile_rows(key, part):
    return support_pair(jax.random.fold_in(key, 11))[0]


def draw_tile_cols(key, part):
    return support_pair(jax.random.fold_in(key, 11))[1]


def draw_tile_active(key, part):
    device_count = N_ROW * N_COL
    live_count = jax.random.randint(jax.random.fold_in(key, 23), (device_count,), SLOTS // 3, SLOTS + 1)
    live_count = live_count.at[0].set(SLOTS)
    slots_iota = jnp.arange(SLOTS, dtype=jnp.int32)
    mask_all = (slots_iota[None, :] < live_count[:, None]).astype(jnp.int32)
    return mask_all.reshape(N_ROW, N_COL, SLOTS)


def draw_omega_diag(key, part):
    block_count = N_ROW * N_COL
    first_key = jax.random.fold_in(key, 31)
    second_key = jax.random.fold_in(key, 37)
    off_part = jax.random.normal(first_key, (block_count, B, B), jnp.float32)
    logs = jax.random.uniform(second_key, (block_count, B), jnp.float32, jnp.log(0.6), jnp.log(3.5))
    off_part = (off_part + jnp.transpose(off_part, (0, 2, 1))) * 0.70710678
    identity = jnp.eye(B, dtype=jnp.float32)
    tiles_all = off_part * (1.0 - identity[None]) + identity[None] * jnp.exp(logs)[:, None, :]
    return tiles_all.reshape(block_count * B, B).astype(jnp.float32)


def shard_levels(rng, shape, pieces, smallest, largest):
    loudness = 1.0
    for axis_at, shards_of in pieces:
        heights = jax.random.uniform(jax.random.fold_in(jax.random.fold_in(rng, 6), axis_at), (shards_of,), jnp.float32, smallest / len(pieces), largest / len(pieces))
        loudness = loudness * jnp.repeat(jnp.exp(heights), shape[axis_at] // shards_of).reshape((-1,) + (1,) * (len(shape) - 1 - axis_at))
    return loudness


def normal_values(stream_key, shape, spread, most, split=(), kind=jnp.bfloat16):
    array = jax.random.normal(stream_key, shape, jnp.float32) * spread
    if len(split) > 0:
        array = shard_levels(stream_key, shape, split, -0.22, 0.18) * array
    return jnp.clip(array, min=-most, max=most).astype(kind)


def setup_inputs(seed: int = 0) -> dict:
    key_of = jax.random.split(jax.random.key(seed), 7)
    samples = normal_values(key_of[0], (NSAMP, P_SIZE), 1.0, 6.0, ((1, 32),), jnp.float32)
    omega_tiles = normal_values(key_of[1], (N_ROW, N_COL, SLOTS, B, B), 1.0, 6.0, ((0, 4), (1, 8)), jnp.float32)
    omega_diag = draw_omega_diag(jax.random.fold_in(key_of[6], 71), 0)
    tile_rows = draw_tile_rows(jax.random.fold_in(key_of[6], 71), 0)
    tile_cols = draw_tile_cols(jax.random.fold_in(key_of[6], 71), 0)
    tile_active = draw_tile_active(jax.random.fold_in(key_of[6], 71), 0)
    return dict(samples=samples, omega_tiles=omega_tiles, omega_diag=omega_diag, tile_rows=tile_rows, tile_cols=tile_cols, tile_active=tile_active)


HIGHEST = lax.Precision.HIGHEST
STEP_SIZE = 0.05
PENALTY = 4.0


def soft_shrink(values, limit):
    return jnp.sign(values) * jnp.maximum(jnp.abs(values) - limit, 0.0)


def reference(samples, omega_tiles, omega_diag, tile_rows, tile_cols, tile_active):
    block_count = N_ROW * N_COL
    blocks = jnp.transpose(samples.reshape(NSAMP, block_count, B), (1, 0, 2))
    devices = jnp.arange(block_count, dtype=jnp.int32)
    global_rows = ((devices // N_COL)[:, None] * N_COL + tile_rows.reshape(block_count, SLOTS)).astype(jnp.int32)
    global_cols = (tile_cols.reshape(block_count, SLOTS) * N_COL + (devices % N_COL)[:, None]).astype(jnp.int32)
    active_all = tile_active.reshape(block_count, SLOTS)
    tile_set = omega_tiles.reshape(block_count, SLOTS, B, B)
    diag_tiles = omega_diag.reshape(block_count, B, B)
    z_start = jnp.einsum('dnk,dkl->dnl', blocks, diag_tiles, precision=HIGHEST)

    def accumulate(z_total, element):
        tiles_here, rows_here, cols_here = element
        z_total = z_total.at[cols_here].add(jnp.einsum('snk,skl->snl', blocks[rows_here], tiles_here, precision=HIGHEST))
        z_total = z_total.at[rows_here].add(jnp.einsum('snl,skl->snk', blocks[cols_here], tiles_here, precision=HIGHEST))
        return z_total, None

    z_full, _ = lax.scan(accumulate, z_start, (tile_set, global_rows, global_cols))

    def update(state, element):
        tiles_here, rows_here, cols_here, active_here = element
        gradient = jnp.einsum('snk,snl->skl', blocks[rows_here], z_full[cols_here], precision=HIGHEST)
        gradient = gradient + jnp.einsum('snk,snl->skl', z_full[rows_here], blocks[cols_here], precision=HIGHEST)
        gradient = gradient / (2.0 * NSAMP)
        stepped = tiles_here - STEP_SIZE * gradient
        updated = jnp.where(active_here[:, None, None] > 0, soft_shrink(stepped, STEP_SIZE * PENALTY), tiles_here)
        return state, updated

    _, new_tiles = lax.scan(update, jnp.zeros((), jnp.float32), (tile_set, global_rows, global_cols, active_all))
    inverse = 1.0 / jnp.diagonal(diag_tiles, axis1=1, axis2=2)
    identity = jnp.eye(B, dtype=jnp.float32)
    diag_grad = jnp.einsum('dnk,dnl->dkl', blocks, z_full, precision=HIGHEST)
    diag_grad = diag_grad + jnp.einsum('dnk,dnl->dkl', z_full, blocks, precision=HIGHEST)
    diag_grad = diag_grad / (2.0 * NSAMP) - identity[None] * inverse[:, None, :]
    diag_step = diag_tiles - STEP_SIZE * diag_grad
    new_diag = jnp.where(identity[None] > 0, diag_step, soft_shrink(diag_step, STEP_SIZE * PENALTY))
    return new_tiles.reshape(N_ROW, N_COL, SLOTS, B, B), new_diag.reshape(P_SIZE, B)
```

```python
import functools

import jax
import jax.numpy as jnp
from jax import lax
from jax.experimental import pallas as pl
from jax.experimental.pallas import tpu as pltpu
from jax.sharding import PartitionSpec as P

STEP_SIZE = 0.05
PENALTY = 4.0
F32 = jnp.float32
BF16 = jnp.bfloat16
VMEM_BYTES = 56 * 1024 * 1024
NN = (((1,), (0,)), ((), ()))
NT = (((1,), (1,)), ((), ()))


def split(values):
    high = values.astype(BF16)
    return high, (values - high.astype(F32)).astype(BF16)


def dot3(left, right, dims):
    (lh, ll), (rh, rl) = left, right
    mul = functools.partial(lax.dot_general, dimension_numbers=dims, preferred_element_type=F32)
    return mul(lh, rh) + (mul(ll, rh) + mul(lh, rl))


def shrink(values, limit):
    return jnp.maximum(values - limit, 0.0) + jnp.minimum(values + limit, 0.0)


def ring_place(index, count):
    return jnp.where(index % 2 == 0, index // 2, count - 1 - index // 2)


def behind(index, count):
    return lax.rem(ring_place(lax.axis_index("col"), count) - ring_place(index, count) + count, count)


def ahead(index, count):
    return lax.rem(ring_place(index, count) - ring_place(lax.axis_index("col"), count) + count, count)


def row_slot(index, count, sign):
    me = lax.axis_index("row")
    pairs = count // 2
    apart = lax.rem(sign * (me // 2 - index // 2) + pairs, pairs)
    return 2 * apart + lax.rem(me + index, 2)


def w_kernel(nr, nc, rows, cols, *refs):
    x_refs, refs = refs[: 2 * nr], refs[2 * nr :]
    t_ref, refs = refs[0], refs[1:]
    out_refs, (xh, xl, acc) = refs[: 2 * nc], refs[2 * nc :]
    half = x_refs[0].shape[0]
    slot = pl.program_id(0)

    @pl.when(slot == 0)
    def _():
        for k in range(2 * nr):
            at = pl.ds((k % 2) * half, half)
            xh[k // 2, at, :], xl[k // 2, at, :] = split(x_refs[k][...])
        acc[...] = jnp.zeros_like(acc)

    j = row_slot(cols[slot], nr, 1)
    i = ahead(rows[slot], nc)
    acc[i] += dot3((xh[j], xl[j]), split(t_ref[0, 0, 0]), NT)

    @pl.when(slot == pl.num_programs(0) - 1)
    def _():
        for k in range(2 * nc):
            out_refs[k][...] = acc[k // 2, pl.ds((k % 2) * half, half), :]


def y_kernel(nr, nc, rows, cols, *refs):
    x_refs, refs = refs[: 2 * nc], refs[2 * nc :]
    (t_ref, d_ref), refs = refs[:2], refs[2:]
    out_refs, (xh, xl, acc) = refs[:nr], refs[nr:]
    half = x_refs[0].shape[0]
    slot = pl.program_id(0)

    @pl.when(slot == 0)
    def _():
        for k in range(2 * nc):
            at = pl.ds((k % 2) * half, half)
            xh[k // 2, at, :], xl[k // 2, at, :] = split(x_refs[k][...])
        acc[...] = jnp.zeros_like(acc)
        acc[0] = dot3((xh[0], xl[0]), split(d_ref[...]), NN)

    j = row_slot(cols[slot], nr, -1)
    i = behind(rows[slot], nc)
    acc[j] += dot3((xh[i], xl[i]), split(t_ref[0, 0, 0]), NN)

    @pl.when(slot == pl.num_programs(0) - 1)
    def _():
        for k in range(nr):
            out_refs[k][...] = acc[k]


def transposed(a_ref, b_ref):
    return split(jnp.concatenate([a_ref[...].T, b_ref[...].T], axis=1))


def a_kernel(nr, nc, scale, rows, cols, *refs):
    x_refs, refs = refs[: 2 * nc], refs[2 * nc :]
    z_refs, refs = refs[: 2 * nr], refs[2 * nr :]
    t_ref, d_ref, out_ref, dout_ref, xh, xl, zh, zl = refs
    half = x_refs[0].shape[0]
    slot = pl.program_id(0)

    @pl.when(slot == 0)
    def _():
        for k in range(nc):
            xh[k], xl[k] = transposed(x_refs[2 * k], x_refs[2 * k + 1])
        for k in range(2 * nr):
            at = pl.ds((k % 2) * half, half)
            zh[k // 2, at, :], zl[k // 2, at, :] = split(z_refs[k][...])
        gradient = dot3((xh[0], xl[0]), (zh[0], zl[0]), NN)
        gradient = (gradient + gradient.T) * scale
        tile = d_ref[...]
        row = lax.broadcasted_iota(jnp.int32, tile.shape, 0)
        on_diagonal = row == lax.broadcasted_iota(jnp.int32, tile.shape, 1)
        gradient = gradient - jnp.where(on_diagonal, 1.0 / jnp.where(on_diagonal, tile, 1.0), 0.0)
        value = tile - STEP_SIZE * gradient
        dout_ref[...] = jnp.where(on_diagonal, value, shrink(value, STEP_SIZE * PENALTY))

    j = row_slot(cols[slot], nr, 1)
    i = behind(rows[slot], nc)
    gradient = dot3((xh[i], xl[i]), (zh[j], zl[j]), NN)
    out_ref[0] = t_ref[0, 0, 0] - (STEP_SIZE * scale) * gradient


def b_kernel(nr, nc, scale, rows, cols, active, *refs):
    z_refs, refs = refs[: 2 * nc], refs[2 * nc :]
    x_refs, refs = refs[: 2 * nr], refs[2 * nr :]
    t_ref, v_ref, out_ref, zh, zl, xh, xl = refs
    half = x_refs[0].shape[0]
    slot = pl.program_id(0)

    @pl.when(slot == 0)
    def _():
        for k in range(nc):
            zh[k], zl[k] = transposed(z_refs[2 * k], z_refs[2 * k + 1])
        for k in range(2 * nr):
            at = pl.ds((k % 2) * half, half)
            xh[k // 2, at, :], xl[k // 2, at, :] = split(x_refs[k][...])

    j = row_slot(cols[slot], nr, 1)
    i = behind(rows[slot], nc)
    gradient = dot3((zh[i], zl[i]), (xh[j], xl[j]), NN)
    value = v_ref[0] - (STEP_SIZE * scale) * gradient
    live = active[slot] > 0
    out_ref[0, 0, 0] = jnp.where(live, shrink(value, STEP_SIZE * PENALTY), t_ref[0, 0, 0])


def per_device(samples, omega_tiles, omega_diag, tile_rows, tile_cols, tile_active):
    nr = lax.axis_size("row")
    nc = lax.axis_size("col")
    count, side = samples.shape
    half = count // 2
    slots = omega_tiles.shape[2]
    scale = 1.0 / (2.0 * count)
    rows = tile_rows[0, 0]
    cols = tile_cols[0, 0]
    active = tile_active[0, 0]

    ring = list(range(0, nc, 2)) + list(range(1, nc, 2))[::-1]
    right = [(ring[k], ring[(k + 1) % nc]) for k in range(nc)]
    left = [(b, a) for a, b in right]
    chip = [(k, (k + 2) % nr) for k in range(nr)]
    core = [(k, k ^ 1) for k in range(nr)]
    far = nc // 2
    go = lax.ppermute

    def ring_gather(own):
        found = [[None, None] for _ in range(nc)]
        found[0] = list(own)
        for d in range(1, far + 1):
            for at in (0, 1):
                if d < far or at == 0:
                    found[d][at] = go(found[d - 1][at], "col", right)
                if d < far or at == 1:
                    found[(nc - d) % nc][1 - at if d < far else at] = go(
                        found[(nc - d + 1) % nc][1 - at if d < far else at], "col", left
                    )
        return [a for pair in found for a in pair]

    def ring_sum(parts):
        ahead_, back = [None, None], [None, None]
        for d in range(far, 0, -1):
            for at in (0, 1):
                if d < far or at == 0:
                    term = parts[2 * d + at]
                    term = term if ahead_[at] is None else term + ahead_[at]
                    ahead_[at] = go(term, "col", right)
                bt = 1 - at if d < far else at
                if d < far or at == 1:
                    term = parts[2 * (nc - d) + bt]
                    term = term if back[bt] is None else term + back[bt]
                    back[bt] = go(term, "col", left)
        return [parts[at] + ahead_[at] + back[at] for at in (0, 1)]

    def row_gather(own):
        found = [list(own)]
        for _ in range(nr // 2 - 1):
            found.append([go(a, "row", chip) for a in found[-1]])
        return [
            a for pair in found for a in (*pair, *[go(b, "row", core) for b in pair])
        ]

    def row_sum(parts):
        sums = [parts[2 * k] + go(parts[2 * k + 1], "row", core) for k in range(nr // 2)]
        total = None
        for k in range(nr // 2 - 1, 0, -1):
            total = go(sums[k] if total is None else sums[k] + total, "row", chip)
        return sums[0] if total is None else sums[0] + total

    whole = pl.BlockSpec(memory_space=pltpu.VMEM)
    tile_spec = pl.BlockSpec((1, 1, 1, side, side), lambda s, *_: (0, 0, s, 0, 0))
    slot_spec = pl.BlockSpec((1, side, side), lambda s, *_: (s, 0, 0))

    def call(body, n_scalars, in_specs, out_specs, out_shape, scratch):
        return pl.pallas_call(
            body,
            grid_spec=pltpu.PrefetchScalarGridSpec(
                num_scalar_prefetch=n_scalars,
                grid=(slots,),
                in_specs=in_specs,
                out_specs=out_specs,
                scratch_shapes=scratch,
            ),
            out_shape=out_shape,
            compiler_params=pltpu.CompilerParams(vmem_limit_bytes=VMEM_BYTES),
            cost_estimate=pl.CostEstimate(
                flops=6 * slots * count * side * side,
                bytes_accessed=8 * slots * side * side,
                transcendentals=0,
            ),
        )

    def panel(n):
        return [pltpu.VMEM((n, count, side), BF16)] * 2

    def panel_t(n):
        return [pltpu.VMEM((n, side, count), BF16)] * 2

    own = [samples[:half], samples[half:]]
    half_shape = jax.ShapeDtypeStruct((half, side), F32)
    block_shape = jax.ShapeDtypeStruct((count, side), F32)

    x_row = row_gather(own)
    x_col = ring_gather(own)
    w = call(
        functools.partial(w_kernel, nr, nc),
        2,
        [whole] * (2 * nr) + [tile_spec],
        [whole] * (2 * nc),
        [half_shape] * (2 * nc),
        panel(nr) + [pltpu.VMEM((nc, count, side), F32)],
    )(rows, cols, *x_row, omega_tiles)
    w_own = ring_sum(w)
    y = call(
        functools.partial(y_kernel, nr, nc),
        2,
        [whole] * (2 * nc) + [tile_spec, whole],
        [whole] * nr,
        [block_shape] * nr,
        panel(nc) + [pltpu.VMEM((nr, count, side), F32)],
    )(rows, cols, *x_col, omega_tiles, omega_diag)
    y_own = row_sum(y)
    z = [w_own[0] + y_own[:half], w_own[1] + y_own[half:]]
    z_row = row_gather(z)
    z_col = ring_gather(z)
    partial, new_diag = call(
        functools.partial(a_kernel, nr, nc, scale),
        2,
        [whole] * (2 * nc + 2 * nr) + [tile_spec, whole],
        [slot_spec, whole],
        [
            jax.ShapeDtypeStruct((slots, side, side), F32),
            jax.ShapeDtypeStruct((side, side), F32),
        ],
        panel_t(nc) + panel(nr),
    )(rows, cols, *x_col, *z_row, omega_tiles, omega_diag)
    new_tiles = call(
        functools.partial(b_kernel, nr, nc, scale),
        3,
        [whole] * (2 * nc + 2 * nr) + [tile_spec, slot_spec],
        tile_spec,
        jax.ShapeDtypeStruct(omega_tiles.shape, F32),
        panel_t(nc) + panel(nr),
    )(rows, cols, active, *z_col, *x_row, omega_tiles, partial)
    return new_tiles, new_diag


def solution(mesh):
    in_specs = (
        P(None, ("row", "col")),
        P("row", "col", None, None, None),
        P(("row", "col"), None),
        P("row", "col", None),
        P("row", "col", None),
        P("row", "col", None),
    )
    out_specs = (P("row", "col", None, None, None), P(("row", "col"), None))
    return jax.shard_map(
        per_device, mesh=mesh, in_specs=in_specs, out_specs=out_specs, check_vma=False
    )
```

```python
import functools

import jax
import jax.numpy as jnp
from jax import lax
from jax.experimental import pallas as pl
from jax.experimental.pallas import tpu as pltpu
from jax.sharding import PartitionSpec as P

STEP_SIZE = 0.05
PENALTY = 4.0
F32 = jnp.float32
BF16 = jnp.bfloat16
VMEM_BYTES = 32 * 1024 * 1024
COST_BYTES = 20_000_000
NN = (((1,), (0,)), ((), ()))
NT = (((1,), (1,)), ((), ()))


def split(values):
    high = values.astype(BF16)
    return high, (values - high.astype(F32)).astype(BF16)


def dot3(left, right, dims):
    (lh, ll), (rh, rl) = left, right
    mul = functools.partial(lax.dot_general, dimension_numbers=dims, preferred_element_type=F32)
    return mul(lh, rh) + (mul(ll, rh) + mul(lh, rl))


def shrink(values, limit):
    return jnp.maximum(values - limit, 0.0) + jnp.minimum(values + limit, 0.0)


def ring_place(index, count):
    return jnp.where(index % 2 == 0, index // 2, count - 1 - index // 2)


def behind(index, count):
    return lax.rem(ring_place(lax.axis_index("col"), count) - ring_place(index, count) + count, count)


def ahead(index, count):
    return lax.rem(ring_place(index, count) - ring_place(lax.axis_index("col"), count) + count, count)


def row_slot(index, count, sign):
    me = lax.axis_index("row")
    pairs = count // 2
    apart = lax.rem(sign * (me // 2 - index // 2) + pairs, pairs)
    return 2 * apart + lax.rem(me + index, 2)


def fill(refs, high, low):
    for k, ref in enumerate(refs):
        high[k], low[k] = split(ref[...])


def fill_turned(refs, high, low):
    for k, ref in enumerate(refs):
        high[k], low[k] = split(ref[...].T)


def w_kernel(nr, nc, rows, cols, t_ref, *refs):
    x_refs, out_refs, (xh, xl, acc) = refs[:nr], refs[nr : nr + nc], refs[nr + nc :]
    fill(x_refs, xh, xl)
    acc[...] = jnp.zeros_like(acc)
    for slot in range(t_ref.shape[2]):
        j = row_slot(cols[0, 0, slot], nr, 1)
        i = ahead(rows[0, 0, slot], nc)
        acc[i] += dot3((xh[j], xl[j]), split(t_ref[0, 0, slot]), NT)
    for k in range(nc):
        out_refs[k][...] = acc[k]


def y_kernel(nr, nc, rows, cols, t_ref, d_ref, *refs):
    x_refs, out_refs, (xh, xl, acc) = refs[:nc], refs[nc : nc + nr], refs[nc + nr :]
    fill(x_refs, xh, xl)
    acc[...] = jnp.zeros_like(acc)
    acc[0] = dot3((xh[0], xl[0]), split(d_ref[...]), NN)
    for slot in range(t_ref.shape[2]):
        j = row_slot(cols[0, 0, slot], nr, -1)
        i = behind(rows[0, 0, slot], nc)
        acc[j] += dot3((xh[i], xl[i]), split(t_ref[0, 0, slot]), NN)
    for k in range(nr):
        out_refs[k][...] = acc[k]


def a_kernel(nr, nc, scale, rows, cols, t_ref, d_ref, *refs):
    x_refs, z_refs, refs = refs[:nc], refs[nc : nc + nr], refs[nc + nr :]
    out_ref, dout_ref, xh, xl, zh, zl = refs
    fill_turned(x_refs, xh, xl)
    fill(z_refs, zh, zl)
    gradient = dot3((xh[0], xl[0]), (zh[0], zl[0]), NN)
    gradient = (gradient + gradient.T) * scale
    tile = d_ref[...]
    row = lax.broadcasted_iota(jnp.int32, tile.shape, 0)
    on_diagonal = row == lax.broadcasted_iota(jnp.int32, tile.shape, 1)
    gradient = gradient - jnp.where(on_diagonal, 1.0 / jnp.where(on_diagonal, tile, 1.0), 0.0)
    value = tile - STEP_SIZE * gradient
    dout_ref[...] = jnp.where(on_diagonal, value, shrink(value, STEP_SIZE * PENALTY))
    for slot in range(t_ref.shape[2]):
        j = row_slot(cols[0, 0, slot], nr, 1)
        i = behind(rows[0, 0, slot], nc)
        gradient = dot3((xh[i], xl[i]), (zh[j], zl[j]), NN)
        out_ref[slot] = t_ref[0, 0, slot] - (STEP_SIZE * scale) * gradient


def b_kernel(nr, nc, scale, rows, cols, active, t_ref, v_ref, *refs):
    z_refs, x_refs, refs = refs[:nc], refs[nc : nc + nr], refs[nc + nr :]
    out_ref, zh, zl, xh, xl, made, sems = refs
    fill_turned(z_refs, zh, zl)
    fill(x_refs, xh, xl)
    copies = []
    for slot in range(t_ref.shape[2]):
        j = row_slot(cols[0, 0, slot], nr, 1)
        i = behind(rows[0, 0, slot], nc)
        gradient = dot3((zh[i], zl[i]), (xh[j], xl[j]), NN)
        value = shrink(v_ref[slot] - (STEP_SIZE * scale) * gradient, STEP_SIZE * PENALTY)
        made[slot] = jnp.where(active[0, 0, slot] > 0, value, t_ref[0, 0, slot])
        copies.append(pltpu.make_async_copy(made.at[slot], out_ref.at[0, 0, slot], sems.at[slot]))
        copies[-1].start()
    for copy in copies:
        copy.wait()


def per_device(samples, omega_tiles, omega_diag, tile_rows, tile_cols, tile_active):
    nr = lax.axis_size("row")
    nc = lax.axis_size("col")
    count, side = samples.shape
    slots = omega_tiles.shape[2]
    scale = 1.0 / (2.0 * count)
    even_core = lax.axis_index("row") % 2 == 0

    ring = list(range(0, nc, 2)) + list(range(1, nc, 2))[::-1]
    right = [(ring[k], ring[(k + 1) % nc]) for k in range(nc)]
    left = [(b, a) for a, b in right]
    chip = [(k, (k + 2) % nr) for k in range(nr)]
    core = [(k, k ^ 1) for k in range(nr)]
    both = [
        (r * nc + a, r * nc + b) for r in range(nr) for a, b in (right if r % 2 == 0 else left)
    ]
    far = nc // 2
    go = lax.ppermute

    def ring_gather(own):
        found = [own] + [None] * (nc - 1)
        for d in range(1, far):
            found[d] = go(found[d - 1], "col", right)
            found[nc - d] = go(found[(nc - d + 1) % nc], "col", left)
        found[far] = go(jnp.where(even_core, found[far - 1], found[far + 1]), ("row", "col"), both)
        return found

    def ring_sum(parts):
        first = go(parts[far], ("row", "col"), both)
        one = jnp.where(even_core, parts[far - 1] + first, parts[far - 1])
        two = jnp.where(even_core, parts[far + 1], parts[far + 1] + first)
        for d in range(far - 1, 0, -1):
            one = go(one, "col", right)
            two = go(two, "col", left)
            if d > 1:
                one = parts[d - 1] + one
                two = parts[nc - d + 1] + two
        return parts[0], one, two

    def row_gather(own):
        found = [own]
        for _ in range(nr // 2 - 1):
            found.append(go(found[-1], "row", chip))
        return [a for b in found for a in (b, go(b, "row", core))]

    def row_sum(parts):
        sums = [parts[2 * k] + go(parts[2 * k + 1], "row", core) for k in range(nr // 2)]
        total = None
        for k in range(nr // 2 - 1, 0, -1):
            total = go(sums[k] if total is None else sums[k] + total, "row", chip)
        return (sums[0],) if total is None else (sums[0], total)

    scalars = pl.BlockSpec(memory_space=pltpu.SMEM)
    whole = pl.BlockSpec(memory_space=pltpu.VMEM)

    def call(body, n_scalars, n_in, out_specs, out_shape, scratch):
        return pl.pallas_call(
            body,
            in_specs=[scalars] * n_scalars + [whole] * n_in,
            out_specs=out_specs,
            out_shape=out_shape,
            scratch_shapes=scratch,
            compiler_params=pltpu.CompilerParams(vmem_limit_bytes=VMEM_BYTES),
            cost_estimate=pl.CostEstimate(
                flops=6 * slots * count * side * side, bytes_accessed=COST_BYTES, transcendentals=0
            ),
        )

    def panel(n):
        return [pltpu.VMEM((n, count, side), BF16)] * 2

    def panel_t(n):
        return [pltpu.VMEM((n, side, count), BF16)] * 2

    block = jax.ShapeDtypeStruct((count, side), F32)
    tiles = jax.ShapeDtypeStruct((slots, side, side), F32)

    x_col = ring_gather(samples)
    x_row = row_gather(samples)
    w = call(
        functools.partial(w_kernel, nr, nc),
        2,
        1 + nr,
        [whole] * nc,
        [block] * nc,
        panel(nr) + [pltpu.VMEM((nc, count, side), F32)],
    )(tile_rows, tile_cols, omega_tiles, *x_row)
    w_own = ring_sum(w)
    y = call(
        functools.partial(y_kernel, nr, nc),
        2,
        2 + nc,
        [whole] * nr,
        [block] * nr,
        panel(nc) + [pltpu.VMEM((nr, count, side), F32)],
    )(tile_rows, tile_cols, omega_tiles, omega_diag, *x_col)
    z = sum(row_sum(y)[::-1] + w_own)
    z_col = ring_gather(z)
    z_row = row_gather(z)
    partial, new_diag = call(
        functools.partial(a_kernel, nr, nc, scale),
        2,
        2 + nc + nr,
        [whole] * 2,
        [tiles, jax.ShapeDtypeStruct((side, side), F32)],
        panel_t(nc) + panel(nr),
    )(tile_rows, tile_cols, omega_tiles, omega_diag, *x_col, *z_row)
    new_tiles = call(
        functools.partial(b_kernel, nr, nc, scale),
        3,
        2 + nc + nr,
        pl.BlockSpec(memory_space=pl.ANY),
        jax.ShapeDtypeStruct(omega_tiles.shape, F32),
        panel_t(nc) + panel(nr) + [pltpu.VMEM((slots, side, side), F32), pltpu.SemaphoreType.DMA((slots,))],
    )(tile_rows, tile_cols, tile_active, omega_tiles, partial, *z_col, *x_row)
    return new_tiles, new_diag


def solution(mesh):
    in_specs = (
        P(None, ("row", "col")),
        P("row", "col", None, None, None),
        P(("row", "col"), None),
        P("row", "col", None),
        P("row", "col", None),
        P("row", "col", None),
    )
    out_specs = (P("row", "col", None, None, None), P(("row", "col"), None))
    return jax.shard_map(
        per_device, mesh=mesh, in_specs=in_specs, out_specs=out_specs, check_vma=False
    )
```

```python
import functools

import jax
import jax.numpy as jnp
from jax import lax
from jax.experimental import pallas as pl
from jax.experimental.pallas import tpu as pltpu
from jax.sharding import PartitionSpec as P

STEP_SIZE = 0.05
PENALTY = 4.0
F32 = jnp.float32
BF16 = jnp.bfloat16
COST_BYTES = 20_000_000
GROUP = 5
NN = (((1,), (0,)), ((), ()))
NT = (((1,), (1,)), ((), ()))


def split(values):
    high = values.astype(BF16)
    return high, (values - high.astype(F32)).astype(BF16)


def dot3(left, right, dims):
    (lh, ll), (rh, rl) = left, right
    mul = functools.partial(lax.dot_general, dimension_numbers=dims, preferred_element_type=F32)
    return mul(lh, rh) + (mul(ll, rh) + mul(lh, rl))


def shrink(values, limit):
    return jnp.maximum(values - limit, 0.0) + jnp.minimum(values + limit, 0.0)


def wrapped(index, count):
    return jnp.where(index < 0, index + count, index)


def ring_place(index, count):
    return jnp.where(index & 1 == 0, index >> 1, count - 1 - (index >> 1))


def behind(index, count):
    return wrapped(ring_place(lax.axis_index("col"), count) - ring_place(index, count), count)


def ahead(index, count):
    return wrapped(ring_place(index, count) - ring_place(lax.axis_index("col"), count), count)


def row_slot(index, count, sign):
    me = lax.axis_index("row")
    return 2 * wrapped(sign * ((me >> 1) - (index >> 1)), count // 2) + ((me + index) & 1)


def fill(refs, high, low):
    for k, ref in enumerate(refs):
        high[k], low[k] = split(ref[...])


def fill_turned(refs, high, low):
    for k, ref in enumerate(refs):
        high[k], low[k] = split(ref[...].T)


def fetch(sources, targets, sems):
    copies = [
        pltpu.make_async_copy(a.at[0, 0] if len(a.shape) == 3 else a, b, sems.at[k])
        for k, (a, b) in enumerate(zip(sources, targets))
    ]
    for copy in copies:
        copy.start()
    return copies


def w_kernel(nr, nc, rows_in, cols_in, t_in, *refs):
    x_refs, out_refs, refs = refs[:nr], refs[nr : nr + nc], refs[nr + nc :]
    t_ref, rows, cols, sems, t_sems, out_sems, xh, xl, acc = refs
    small = fetch((rows_in, cols_in), (rows, cols), sems)
    groups = []
    for k in range(t_ref.shape[0] // GROUP):
        at = pl.ds(k * GROUP, GROUP)
        groups.append(pltpu.make_async_copy(t_in.at[0, 0, at], t_ref.at[at], t_sems.at[k]))
        groups[-1].start()
    fill(x_refs, xh, xl)
    acc[...] = jnp.zeros_like(acc)
    for copy in small:
        copy.wait()
    for slot in range(t_ref.shape[0]):
        if slot % GROUP == 0:
            groups[slot // GROUP].wait()
        j = row_slot(cols[slot], nr, 1)
        i = ahead(rows[slot], nc)
        acc[i] += dot3((xh[j], xl[j]), split(t_ref[slot]), NT)
    copies = [pltpu.make_async_copy(acc.at[k], out_refs[k], out_sems.at[k]) for k in range(nc)]
    for copy in copies:
        copy.start()
    for copy in copies:
        copy.wait()


def y_kernel(nr, nc, rows_in, cols_in, d_in, t_ref, *refs):
    x_refs, out_refs, refs = refs[:nc], refs[nc : nc + nr], refs[nc + nr :]
    rows, cols, d_ref, sems, xh, xl, acc = refs
    small = fetch((rows_in, cols_in, d_in), (rows, cols, d_ref), sems)
    fill(x_refs, xh, xl)
    acc[...] = jnp.zeros_like(acc)
    for copy in small:
        copy.wait()
    acc[0] = dot3((xh[0], xl[0]), split(d_ref[...]), NN)
    for slot in range(t_ref.shape[0]):
        j = row_slot(cols[slot], nr, -1)
        i = behind(rows[slot], nc)
        acc[j] += dot3((xh[i], xl[i]), split(t_ref[slot]), NN)
    for k in range(nr):
        out_refs[k][...] = acc[k]


def prepare_kernel(nr, nc, *refs):
    x_refs, r_refs, (th, tl, rh, rl) = refs[:nc], refs[nc : nc + nr], refs[nc + nr :]
    fill_turned(x_refs, th, tl)
    fill(r_refs, rh, rl)


def first_kernel(nr, nc, scale, rows_in, cols_in, live_in, d_in, t_ref, th, tl, *refs):
    z_refs, refs = refs[:nr], refs[nr:]
    out_ref, dout_ref, rows, cols, live, d_ref, sems, zh, zl = refs
    small = fetch((rows_in, cols_in, live_in, d_in), (rows, cols, live, d_ref), sems)
    fill(z_refs, zh, zl)
    for copy in small:
        copy.wait()
    gradient = dot3((th[0], tl[0]), (zh[0], zl[0]), NN)
    gradient = (gradient + gradient.T) * scale
    tile = d_ref[...]
    row = lax.broadcasted_iota(jnp.int32, tile.shape, 0)
    on_diagonal = row == lax.broadcasted_iota(jnp.int32, tile.shape, 1)
    gradient = gradient - jnp.where(on_diagonal, 1.0 / jnp.where(on_diagonal, tile, 1.0), 0.0)
    value = tile - STEP_SIZE * gradient
    dout_ref[...] = jnp.where(on_diagonal, value, shrink(value, STEP_SIZE * PENALTY))
    for slot in range(t_ref.shape[0]):
        j = row_slot(cols[slot], nr, 1)
        i = behind(rows[slot], nc)
        gradient = dot3((th[i], tl[i]), (zh[j], zl[j]), NN)
        out_ref[slot] = t_ref[slot] - jnp.where(live[slot] > 0, STEP_SIZE * scale, 0.0) * gradient


def second_kernel(nr, nc, scale, places, rows_in, cols_in, live_in, v_ref, rh, rl, *refs):
    z_refs, refs = refs[: len(places)], refs[len(places) :]
    out_ref, made, rows, cols, live, sems, zh, zl, out_sems = refs
    small = fetch((rows_in, cols_in, live_in), (rows, cols, live), sems)
    fill_turned(z_refs, zh, zl)
    for copy in small:
        copy.wait()
    copies, mine = [], []
    for slot in range(v_ref.shape[0]):
        place = behind(rows[slot], nc)
        i = sum(jnp.where(place == p, k, 0) for k, p in enumerate(places))
        mine.append(functools.reduce(jnp.logical_or, [place == p for p in places]))
        copies.append(pltpu.make_async_copy(made.at[slot], out_ref.at[0, 0, slot], out_sems.at[slot]))
        j = row_slot(cols[slot], nr, 1)
        gradient = dot3((zh[i], zl[i]), (rh[j], rl[j]), NN)
        value = v_ref[slot]
        new = shrink(value - (STEP_SIZE * scale) * gradient, STEP_SIZE * PENALTY)
        made[slot] = jnp.where(jnp.logical_and(live[slot] > 0, mine[slot]), new, value)
    for slot in range(v_ref.shape[0]):
        pl.when(mine[slot])(copies[slot].start)
    for slot in range(v_ref.shape[0]):
        pl.when(mine[slot])(copies[slot].wait)


def late_kernel(nr, nc, scale, places, rows_in, cols_in, live_in, v_ref, rh, rl, *refs):
    z_refs, refs = refs[: len(places)], refs[len(places) :]
    _, out_ref, rows, cols, live, sems, zh, zl, made, out_sems = refs
    small = fetch((rows_in, cols_in, live_in), (rows, cols, live), sems)
    fill_turned(z_refs, zh, zl)
    for copy in small:
        copy.wait()
    mine, copies = [], []
    for slot in range(v_ref.shape[0]):
        place = behind(rows[slot], nc)
        i = sum(jnp.where(place == p, k, 0) for k, p in enumerate(places))
        mine.append(functools.reduce(jnp.logical_or, [place == p for p in places]))
        copies.append(pltpu.make_async_copy(made.at[slot], out_ref.at[0, 0, slot], out_sems.at[slot]))

        @pl.when(mine[slot])
        def _():
            j = row_slot(cols[slot], nr, 1)
            gradient = dot3((zh[i], zl[i]), (rh[j], rl[j]), NN)
            value = v_ref[slot]
            new = shrink(value - (STEP_SIZE * scale) * gradient, STEP_SIZE * PENALTY)
            made[slot] = jnp.where(live[slot] > 0, new, value)
            copies[slot].start()

    for slot in range(v_ref.shape[0]):
        pl.when(mine[slot])(copies[slot].wait)


def per_device(samples, omega_tiles, omega_diag, tile_rows, tile_cols, tile_active):
    nr = lax.axis_size("row")
    nc = lax.axis_size("col")
    count, side = samples.shape
    slots = omega_tiles.shape[2]
    scale = 1.0 / (2.0 * count)
    even_core = lax.axis_index("row") % 2 == 0

    ring = list(range(0, nc, 2)) + list(range(1, nc, 2))[::-1]
    right = [(ring[k], ring[(k + 1) % nc]) for k in range(nc)]
    left = [(b, a) for a, b in right]
    chip = [(k, (k + 2) % nr) for k in range(nr)]
    core = [(k, k ^ 1) for k in range(nr)]
    both = [
        (r * nc + a, r * nc + b) for r in range(nr) for a, b in (right if r % 2 == 0 else left)
    ]
    far = nc // 2
    go = lax.ppermute

    def ring_gather(own, beside):
        found = [own] + [None] * (nc - 1)
        for d in range(1, far + 1):
            one, two = found[d - 1], found[(nc - d + 1) % nc]
            if d in beside:
                one, two, _ = lax.optimization_barrier((one, two, beside[d](found)))
            if d < far:
                found[d] = go(one, "col", right)
                found[nc - d] = go(two, "col", left)
            else:
                found[far] = go(jnp.where(even_core, one, two), ("row", "col"), both)
        return found

    def ring_sum(parts):
        first = go(parts[far], ("row", "col"), both)
        one = jnp.where(even_core, parts[far - 1] + first, parts[far - 1])
        two = jnp.where(even_core, parts[far + 1], parts[far + 1] + first)
        for d in range(far - 1, 0, -1):
            one = go(one, "col", right)
            two = go(two, "col", left)
            if d > 1:
                one = parts[d - 1] + one
                two = parts[nc - d + 1] + two
        return parts[0], one, two

    def row_gather(own):
        found = [own]
        for _ in range(nr // 2 - 1):
            found.append(go(found[-1], "row", chip))
        return [a for b in found for a in (b, go(b, "row", core))]

    def row_sum(parts):
        sums = [parts[2 * k] + go(parts[2 * k + 1], "row", core) for k in range(nr // 2)]
        total = None
        for k in range(nr // 2 - 1, 0, -1):
            total = go(sums[k] if total is None else sums[k] + total, "row", chip)
        return (sums[0],) if total is None else (sums[0], total)

    whole = pl.BlockSpec(memory_space=pltpu.VMEM)
    in_place = pl.BlockSpec(memory_space=pltpu.HBM)

    def call(body, n_hbm, n_vmem, out_specs, out_shape, scratch, megabytes, aliases=None):
        return pl.pallas_call(
            body,
            in_specs=[in_place] * n_hbm + [whole] * n_vmem + [in_place] * len(aliases or {}),
            out_specs=out_specs,
            out_shape=out_shape,
            scratch_shapes=scratch,
            input_output_aliases=aliases or {},
            compiler_params=pltpu.CompilerParams(vmem_limit_bytes=megabytes * 1024 * 1024),
            cost_estimate=pl.CostEstimate(
                flops=6 * slots * count * side * side, bytes_accessed=COST_BYTES, transcendentals=0
            ),
        )

    def ids(n):
        return [pltpu.SMEM((slots,), jnp.int32)] * n

    def sems(n):
        return pltpu.SemaphoreType.DMA((n,))

    def panel(n):
        return [pltpu.VMEM((n, count, side), BF16)] * 2

    def panel_t(n):
        return [pltpu.VMEM((n, side, count), BF16)] * 2

    block = jax.ShapeDtypeStruct((count, side), F32)
    tile = jax.ShapeDtypeStruct((side, side), F32)
    tiles = jax.ShapeDtypeStruct((slots, side, side), F32)
    turned = jax.ShapeDtypeStruct((nc, side, count), BF16)
    straight = jax.ShapeDtypeStruct((nr, count, side), BF16)

    in_hbm = functools.partial(pltpu.with_memory_space_constraint, memory_space=pltpu.HBM)
    tile_rows, tile_cols, tile_active, omega_tiles, omega_diag = map(
        in_hbm, (tile_rows, tile_cols, tile_active, omega_tiles, omega_diag)
    )
    x_row = row_gather(samples)
    *w, held = call(
        functools.partial(w_kernel, nr, nc),
        3,
        nr,
        [in_place] * nc + [whole],
        [pltpu.HBM((count, side), F32)] * nc + [tiles],
        ids(2) + [sems(2), sems(slots // GROUP), sems(nc)] + panel(nr) + [pltpu.VMEM((nc, count, side), F32)],
        10 + nc,
    )(tile_rows, tile_cols, omega_tiles, *x_row)
    x_col = ring_gather(samples, {far - 1: lambda found: w[0]})
    w_own = ring_sum(w)
    y = call(
        functools.partial(y_kernel, nr, nc),
        3,
        1 + nc,
        [whole] * nr,
        [block] * nr,
        ids(2) + [pltpu.VMEM((side, side), F32), sems(3)] + panel(nc) + [pltpu.VMEM((nr, count, side), F32)],
        10 + nc,
    )(tile_rows, tile_cols, omega_diag, held, *x_col)
    z = sum(row_sum(y)[::-1] + w_own)
    th, tl, rh, rl = call(
        functools.partial(prepare_kernel, nr, nc),
        0,
        nc + nr,
        [whole] * 4,
        [turned] * 2 + [straight] * 2,
        [],
        8,
    )(*x_col, *x_row)
    z, th, tl, rh, rl = lax.optimization_barrier((z, th, tl, rh, rl))
    z_row = row_gather(z)
    made = []

    def first(found):
        made.extend(
            call(
                functools.partial(first_kernel, nr, nc, scale),
                4,
                3 + nr,
                [whole] * 2,
                [tiles, tile],
                ids(3) + [pltpu.VMEM((side, side), F32), sems(4)] + panel(nr),
                10 + nc,
            )(tile_rows, tile_cols, tile_active, omega_diag, held, th, tl, *z_row)
        )
        return made[0]

    def second(found):
        places = sum(steps[:-2], [])
        made.extend(
            call(
                functools.partial(second_kernel, nr, nc, scale, places),
                3,
                3 + len(places),
                [in_place, whole],
                [jax.ShapeDtypeStruct(omega_tiles.shape, F32), tiles],
                ids(3) + [sems(3)] + panel_t(len(places)) + [sems(slots)],
                10 + nc,
            )(tile_rows, tile_cols, tile_active, made[0], rh, rl, *[found[p] for p in places])
        )
        return made[-1]

    steps = [[0], *[[d, nc - d] for d in range(1, far)], [far]]
    z_col = ring_gather(z, {far - 1: first, far: second})
    _, new_diag, new_tiles, partial = made
    for places in steps[-2:]:
        new_tiles = call(
            functools.partial(late_kernel, nr, nc, scale, places),
            3,
            3 + len(places),
            in_place,
            jax.ShapeDtypeStruct(omega_tiles.shape, F32),
            ids(3)
            + [sems(3)]
            + panel_t(len(places))
            + [pltpu.VMEM((slots, side, side), F32), sems(slots)],
            10 + nc,
            {6 + len(places): 0},
        )(tile_rows, tile_cols, tile_active, partial, rh, rl, *[z_col[p] for p in places], new_tiles)
    return new_tiles, new_diag


def solution(mesh):
    in_specs = (
        P(None, ("row", "col")),
        P("row", "col", None, None, None),
        P(("row", "col"), None),
        P("row", "col", None),
        P("row", "col", None),
        P("row", "col", None),
    )
    out_specs = (P("row", "col", None, None, None), P(("row", "col"), None))
    return jax.shard_map(
        per_device, mesh=mesh, in_specs=in_specs, out_specs=out_specs, check_vma=False
    )
```

```python
import functools

import jax
import jax.numpy as jnp
from jax import lax
from jax.experimental import pallas as pl
from jax.experimental.pallas import tpu as pltpu
from jax.sharding import PartitionSpec as P

STEP_SIZE = 0.05
PENALTY = 4.0
F32 = jnp.float32
BF16 = jnp.bfloat16
COST_BYTES = 20_000_000
GROUP = 5
NN = (((1,), (0,)), ((), ()))
NT = (((1,), (1,)), ((), ()))


def split(values):
    high = values.astype(BF16)
    return high, (values - high.astype(F32)).astype(BF16)


def dot3(left, right, dims):
    (lh, ll), (rh, rl) = left, right
    mul = functools.partial(lax.dot_general, dimension_numbers=dims, preferred_element_type=F32)
    return mul(lh, rh) + (mul(ll, rh) + mul(lh, rl))


def shrink(values, limit):
    return jnp.maximum(values - limit, 0.0) + jnp.minimum(values + limit, 0.0)


def wrapped(index, count):
    return jnp.where(index < 0, index + count, index)


def ring_place(index, count):
    return jnp.where(index & 1 == 0, index >> 1, count - 1 - (index >> 1))


def behind(index, count):
    return wrapped(ring_place(lax.axis_index("col"), count) - ring_place(index, count), count)


def ahead(index, count):
    return wrapped(ring_place(index, count) - ring_place(lax.axis_index("col"), count), count)


def row_slot(index, count, sign):
    me = lax.axis_index("row")
    return 2 * wrapped(sign * ((me >> 1) - (index >> 1)), count // 2) + ((me + index) & 1)


def fill(refs, high, low):
    for k, ref in enumerate(refs):
        high[k], low[k] = split(ref[...])


def fill_turned(refs, high, low):
    for k, ref in enumerate(refs):
        high[k], low[k] = split(ref[...].T)


def fetch(sources, targets, sems):
    copies = [
        pltpu.make_async_copy(a.at[0, 0] if len(a.shape) == 3 else a, b, sems.at[k])
        for k, (a, b) in enumerate(zip(sources, targets))
    ]
    for copy in copies:
        copy.start()
    return copies


def w_kernel(nr, nc, near, rows_in, cols_in, own_in, t_in, *refs):
    x_refs, out_refs, refs = refs[: nr - 1], refs[nr - 1 : nr - 1 + nc], refs[nr - 1 + nc :]
    t_ref, rows, cols, own, sems, t_sems, out_sems, xh, xl, acc = refs
    small = fetch((own_in, rows_in, cols_in), (own, rows, cols), sems)
    groups = []
    for k in range(t_ref.shape[0] // GROUP):
        at = pl.ds(k * GROUP, GROUP)
        groups.append(pltpu.make_async_copy(t_in.at[0, 0, at], t_ref.at[at], t_sems.at[k]))
        groups[-1].start()
    for k, ref in enumerate(x_refs):
        xh[k + 1], xl[k + 1] = split(ref[...])
    acc[...] = jnp.zeros_like(acc)
    for copy in small:
        copy.wait()
    xh[0], xl[0] = split(own[...])
    for slot in range(t_ref.shape[0]):
        if slot % GROUP == 0:
            groups[slot // GROUP].wait()
        j = row_slot(cols[slot], nr, 1)
        i = ahead(rows[slot], nc)
        acc[i] += dot3((xh[j], xl[j]), split(t_ref[slot]), NT)
    copies = []
    for k in range(nc):
        if k in near:
            out_refs[k][...] = acc[k]
        else:
            copies.append(pltpu.make_async_copy(acc.at[k], out_refs[k], out_sems.at[k]))
            copies[-1].start()
    for copy in copies:
        copy.wait()


def y_kernel(nr, nc, rows_in, cols_in, d_in, t_ref, *refs):
    x_refs, out_refs, refs = refs[:nc], refs[nc : nc + nr], refs[nc + nr :]
    rows, cols, d_ref, sems, xh, xl, acc = refs
    small = fetch((rows_in, cols_in, d_in), (rows, cols, d_ref), sems)
    fill(x_refs, xh, xl)
    acc[...] = jnp.zeros_like(acc)
    for copy in small:
        copy.wait()
    acc[0] = dot3((xh[0], xl[0]), split(d_ref[...]), NN)
    for slot in range(t_ref.shape[0]):
        j = row_slot(cols[slot], nr, -1)
        i = behind(rows[slot], nc)
        acc[j] += dot3((xh[i], xl[i]), split(t_ref[slot]), NN)
    for k in range(nr):
        out_refs[k][...] = acc[k]


def prepare_kernel(nr, nc, *refs):
    x_refs, r_refs, (th, tl, rh, rl) = refs[:nc], refs[nc : nc + nr], refs[nc + nr :]
    fill_turned(x_refs, th, tl)
    fill(r_refs, rh, rl)


def first_kernel(nr, nc, scale, rows_in, cols_in, live_in, d_in, t_ref, th, tl, *refs):
    z_refs, refs = refs[:nr], refs[nr:]
    out_ref, dout_ref, rows, cols, live, d_ref, sems, zh, zl = refs
    small = fetch((rows_in, cols_in, live_in, d_in), (rows, cols, live, d_ref), sems)
    fill(z_refs, zh, zl)
    for copy in small:
        copy.wait()
    gradient = dot3((th[0], tl[0]), (zh[0], zl[0]), NN)
    gradient = (gradient + gradient.T) * scale
    tile = d_ref[...]
    row = lax.broadcasted_iota(jnp.int32, tile.shape, 0)
    on_diagonal = row == lax.broadcasted_iota(jnp.int32, tile.shape, 1)
    gradient = gradient - jnp.where(on_diagonal, 1.0 / jnp.where(on_diagonal, tile, 1.0), 0.0)
    value = tile - STEP_SIZE * gradient
    dout_ref[...] = jnp.where(on_diagonal, value, shrink(value, STEP_SIZE * PENALTY))
    for slot in range(t_ref.shape[0]):
        j = row_slot(cols[slot], nr, 1)
        i = behind(rows[slot], nc)
        gradient = dot3((th[i], tl[i]), (zh[j], zl[j]), NN)
        out_ref[slot] = t_ref[slot] - jnp.where(live[slot] > 0, STEP_SIZE * scale, 0.0) * gradient


def second_kernel(nr, nc, scale, places, rows_in, cols_in, live_in, v_ref, rh, rl, *refs):
    z_refs, refs = refs[: len(places)], refs[len(places) :]
    out_ref, made, rows, cols, live, sems, zh, zl, out_sems = refs
    small = fetch((rows_in, cols_in, live_in), (rows, cols, live), sems)
    fill_turned(z_refs, zh, zl)
    for copy in small:
        copy.wait()
    copies, mine = [], []
    for slot in range(v_ref.shape[0]):
        place = behind(rows[slot], nc)
        i = sum(jnp.where(place == p, k, 0) for k, p in enumerate(places))
        mine.append(functools.reduce(jnp.logical_or, [place == p for p in places]))
        copies.append(pltpu.make_async_copy(made.at[slot], out_ref.at[0, 0, slot], out_sems.at[slot]))
        j = row_slot(cols[slot], nr, 1)
        gradient = dot3((zh[i], zl[i]), (rh[j], rl[j]), NN)
        value = v_ref[slot]
        new = shrink(value - (STEP_SIZE * scale) * gradient, STEP_SIZE * PENALTY)
        made[slot] = jnp.where(jnp.logical_and(live[slot] > 0, mine[slot]), new, value)
    for slot in range(v_ref.shape[0]):
        pl.when(mine[slot])(copies[slot].start)
    for slot in range(v_ref.shape[0]):
        pl.when(mine[slot])(copies[slot].wait)


def late_kernel(nr, nc, scale, places, rows_in, cols_in, live_in, v_ref, rh, rl, *refs):
    z_refs, refs = refs[: len(places)], refs[len(places) :]
    _, out_ref, rows, cols, live, sems, zh, zl, made, out_sems = refs
    small = fetch((rows_in, cols_in, live_in), (rows, cols, live), sems)
    fill_turned(z_refs, zh, zl)
    for copy in small:
        copy.wait()
    mine, copies = [], []
    for slot in range(v_ref.shape[0]):
        place = behind(rows[slot], nc)
        i = sum(jnp.where(place == p, k, 0) for k, p in enumerate(places))
        mine.append(functools.reduce(jnp.logical_or, [place == p for p in places]))
        copies.append(pltpu.make_async_copy(made.at[slot], out_ref.at[0, 0, slot], out_sems.at[slot]))

        @pl.when(mine[slot])
        def _():
            j = row_slot(cols[slot], nr, 1)
            gradient = dot3((zh[i], zl[i]), (rh[j], rl[j]), NN)
            value = v_ref[slot]
            new = shrink(value - (STEP_SIZE * scale) * gradient, STEP_SIZE * PENALTY)
            made[slot] = jnp.where(live[slot] > 0, new, value)
            copies[slot].start()

    for slot in range(v_ref.shape[0]):
        pl.when(mine[slot])(copies[slot].wait)


def per_device(samples, omega_tiles, omega_diag, tile_rows, tile_cols, tile_active):
    nr = lax.axis_size("row")
    nc = lax.axis_size("col")
    count, side = samples.shape
    slots = omega_tiles.shape[2]
    scale = 1.0 / (2.0 * count)
    even_core = lax.axis_index("row") % 2 == 0

    ring = list(range(0, nc, 2)) + list(range(1, nc, 2))[::-1]
    right = [(ring[k], ring[(k + 1) % nc]) for k in range(nc)]
    left = [(b, a) for a, b in right]
    chip = [(k, (k + 2) % nr) for k in range(nr)]
    core = [(k, k ^ 1) for k in range(nr)]
    both = [
        (r * nc + a, r * nc + b) for r in range(nr) for a, b in (right if r % 2 == 0 else left)
    ]
    far = nc // 2
    go = lax.ppermute

    def ring_gather(own, beside):
        found = [own] + [None] * (nc - 1)
        for d in range(1, far + 1):
            one, two = found[d - 1], found[(nc - d + 1) % nc]
            if d in beside:
                one, two, _ = lax.optimization_barrier((one, two, beside[d](found)))
            if d < far:
                found[d] = go(one, "col", right)
                found[nc - d] = go(two, "col", left)
            else:
                found[far] = go(jnp.where(even_core, one, two), ("row", "col"), both)
        return found

    def ring_sum(parts):
        first = go(parts[far], ("row", "col"), both)
        one = jnp.where(even_core, parts[far - 1] + first, parts[far - 1])
        two = jnp.where(even_core, parts[far + 1], parts[far + 1] + first)
        for d in range(far - 1, 0, -1):
            one = go(one, "col", right)
            two = go(two, "col", left)
            if d > 1:
                one = parts[d - 1] + one
                two = parts[nc - d + 1] + two
        return parts[0], one, two

    def row_gather(own):
        found = [own]
        for _ in range(nr // 2 - 1):
            found.append(go(found[-1], "row", chip))
        return [a for b in found for a in (b, go(b, "row", core))]

    def row_sum(parts):
        sums = [parts[2 * k] + go(parts[2 * k + 1], "row", core) for k in range(nr // 2)]
        total = None
        for k in range(nr // 2 - 1, 0, -1):
            total = go(sums[k] if total is None else sums[k] + total, "row", chip)
        return (sums[0],) if total is None else (sums[0], total)

    whole = pl.BlockSpec(memory_space=pltpu.VMEM)
    in_place = pl.BlockSpec(memory_space=pltpu.HBM)

    def call(body, n_hbm, n_vmem, out_specs, out_shape, scratch, megabytes, aliases=None):
        return pl.pallas_call(
            body,
            in_specs=[in_place] * n_hbm + [whole] * n_vmem + [in_place] * len(aliases or {}),
            out_specs=out_specs,
            out_shape=out_shape,
            scratch_shapes=scratch,
            input_output_aliases=aliases or {},
            compiler_params=pltpu.CompilerParams(vmem_limit_bytes=megabytes * 1024 * 1024),
            cost_estimate=pl.CostEstimate(
                flops=6 * slots * count * side * side, bytes_accessed=COST_BYTES, transcendentals=0
            ),
        )

    def ids(n):
        return [pltpu.SMEM((slots,), jnp.int32)] * n

    def sems(n):
        return pltpu.SemaphoreType.DMA((n,))

    def panel(n):
        return [pltpu.VMEM((n, count, side), BF16)] * 2

    def panel_t(n):
        return [pltpu.VMEM((n, side, count), BF16)] * 2

    block = jax.ShapeDtypeStruct((count, side), F32)
    tile = jax.ShapeDtypeStruct((side, side), F32)
    tiles = jax.ShapeDtypeStruct((slots, side, side), F32)
    turned = jax.ShapeDtypeStruct((nc, side, count), BF16)
    straight = jax.ShapeDtypeStruct((nr, count, side), BF16)

    in_hbm = functools.partial(pltpu.with_memory_space_constraint, memory_space=pltpu.HBM)
    tile_rows, tile_cols, tile_active, omega_tiles, omega_diag = map(
        in_hbm, (tile_rows, tile_cols, tile_active, omega_tiles, omega_diag)
    )
    near = ()
    x_row, w = [], []

    def mirror(found):
        source = samples
        x_row.extend(row_gather(source))
        made_w = call(
            functools.partial(w_kernel, nr, nc, near),
            4,
            nr - 1,
            [whole if k in near else in_place for k in range(nc)] + [whole],
            [block if k in near else pltpu.HBM((count, side), F32) for k in range(nc)] + [tiles],
            ids(2) + [pltpu.VMEM((count, side), F32), sems(3), sems(slots // GROUP), sems(nc)] + panel(nr) + [pltpu.VMEM((nc, count, side), F32)],
            10 + nc,
        )(tile_rows, tile_cols, in_hbm(samples), omega_tiles, *x_row[1:])
        w.extend(made_w)
        return w[0]

    x_col = ring_gather(samples, {far: mirror})
    held = w.pop()
    w_own = ring_sum(w)
    y = call(
        functools.partial(y_kernel, nr, nc),
        3,
        1 + nc,
        [whole] * nr,
        [block] * nr,
        ids(2) + [pltpu.VMEM((side, side), F32), sems(3)] + panel(nc) + [pltpu.VMEM((nr, count, side), F32)],
        10 + nc,
    )(tile_rows, tile_cols, omega_diag, held, *x_col)
    z = sum(row_sum(y)[::-1] + w_own)
    th, tl, rh, rl = call(
        functools.partial(prepare_kernel, nr, nc),
        0,
        nc + nr,
        [whole] * 4,
        [turned] * 2 + [straight] * 2,
        [],
        8,
    )(*x_col, *x_row)
    z, th, tl, rh, rl = lax.optimization_barrier((z, th, tl, rh, rl))
    z_row = row_gather(z)
    made = []

    def first(found):
        made.extend(
            call(
                functools.partial(first_kernel, nr, nc, scale),
                4,
                3 + nr,
                [whole] * 2,
                [tiles, tile],
                ids(3) + [pltpu.VMEM((side, side), F32), sems(4)] + panel(nr),
                10 + nc,
            )(tile_rows, tile_cols, tile_active, omega_diag, held, th, tl, *z_row)
        )
        return made[0]

    def second(found):
        places = sum(steps[:-2], [])
        made.extend(
            call(
                functools.partial(second_kernel, nr, nc, scale, places),
                3,
                3 + len(places),
                [in_place, whole],
                [jax.ShapeDtypeStruct(omega_tiles.shape, F32), tiles],
                ids(3) + [sems(3)] + panel_t(len(places)) + [sems(slots)],
                10 + nc,
            )(tile_rows, tile_cols, tile_active, made[0], rh, rl, *[found[p] for p in places])
        )
        return made[-1]

    steps = [[0], *[[d, nc - d] for d in range(1, far)], [far]]
    z_col = ring_gather(z, {far - 1: first, far: second})
    _, new_diag, new_tiles, partial = made
    for places in steps[-2:]:
        new_tiles = call(
            functools.partial(late_kernel, nr, nc, scale, places),
            3,
            3 + len(places),
            in_place,
            jax.ShapeDtypeStruct(omega_tiles.shape, F32),
            ids(3)
            + [sems(3)]
            + panel_t(len(places))
            + [pltpu.VMEM((slots, side, side), F32), sems(slots)],
            10 + nc,
            {6 + len(places): 0},
        )(tile_rows, tile_cols, tile_active, partial, rh, rl, *[z_col[p] for p in places], new_tiles)
    return new_tiles, new_diag


def solution(mesh):
    in_specs = (
        P(None, ("row", "col")),
        P("row", "col", None, None, None),
        P(("row", "col"), None),
        P("row", "col", None),
        P("row", "col", None),
        P("row", "col", None),
    )
    out_specs = (P("row", "col", None, None, None), P(("row", "col"), None))
    return jax.shard_map(
        per_device, mesh=mesh, in_specs=in_specs, out_specs=out_specs, check_vma=False
    )
```

```python
import functools

import jax
import jax.numpy as jnp
from jax import lax
from jax.experimental import pallas as pl
from jax.experimental.pallas import tpu as pltpu
from jax.sharding import PartitionSpec as P

STEP_SIZE = 0.05
PENALTY = 4.0
F32 = jnp.float32
BF16 = jnp.bfloat16
COST_BYTES = 20_000_000
GROUP = 5
NN = (((1,), (0,)), ((), ()))
NT = (((1,), (1,)), ((), ()))


def split(values):
    high = values.astype(BF16)
    return high, (values - high.astype(F32)).astype(BF16)


def dot3(left, right, dims):
    (lh, ll), (rh, rl) = left, right
    mul = functools.partial(lax.dot_general, dimension_numbers=dims, preferred_element_type=F32)
    return mul(lh, rh) + (mul(ll, rh) + mul(lh, rl))


def shrink(values, limit):
    return jnp.maximum(values - limit, 0.0) + jnp.minimum(values + limit, 0.0)


def wrapped(index, count):
    return jnp.where(index < 0, index + count, index)


def ring_place(index, count):
    return jnp.where(index & 1 == 0, index >> 1, count - 1 - (index >> 1))


def behind(index, count):
    return wrapped(ring_place(lax.axis_index("col"), count) - ring_place(index, count), count)


def ahead(index, count):
    return wrapped(ring_place(index, count) - ring_place(lax.axis_index("col"), count), count)


def row_slot(index, count, sign):
    me = lax.axis_index("row")
    return 2 * wrapped(sign * ((me >> 1) - (index >> 1)), count // 2) + ((me + index) & 1)


def fill(refs, high, low):
    for k, ref in enumerate(refs):
        high[k], low[k] = split(ref[...])


def fill_turned(refs, high, low):
    for k, ref in enumerate(refs):
        high[k], low[k] = split(ref[...].T)


def fetch(sources, targets, sems):
    copies = [
        pltpu.make_async_copy(a.at[0, 0] if len(a.shape) == 3 else a, b, sems.at[k])
        for k, (a, b) in enumerate(zip(sources, targets))
    ]
    for copy in copies:
        copy.start()
    return copies


def w_kernel(nr, nc, near, rows_in, cols_in, own_in, t_in, *refs):
    x_refs, out_refs, refs = refs[: nr - 1], refs[nr - 1 : nr - 1 + nc], refs[nr - 1 + nc :]
    rows, cols, own, t_ref, sems, t_sems, out_sems, xh, xl, acc = refs
    small = fetch((own_in, rows_in, cols_in), (own, rows, cols), sems)
    groups = []
    for k in range(t_ref.shape[0] // GROUP):
        at = pl.ds(k * GROUP, GROUP)
        groups.append(pltpu.make_async_copy(t_in.at[0, 0, at], t_ref.at[at], t_sems.at[k]))
        groups[-1].start()
    for k, ref in enumerate(x_refs):
        xh[k + 1], xl[k + 1] = split(ref[...])
    acc[...] = jnp.zeros_like(acc)
    for copy in small:
        copy.wait()
    xh[0], xl[0] = split(own[...])
    for slot in range(t_ref.shape[0]):
        if slot % GROUP == 0:
            groups[slot // GROUP].wait()
        j = row_slot(cols[slot], nr, 1)
        i = ahead(rows[slot], nc)
        acc[i] += dot3((xh[j], xl[j]), split(t_ref[slot]), NT)
    copies = []
    for k in range(nc):
        if k in near:
            out_refs[k][...] = acc[k]
        else:
            copies.append(pltpu.make_async_copy(acc.at[k], out_refs[k], out_sems.at[k]))
            copies[-1].start()
    for copy in copies:
        copy.wait()


def y_kernel(nr, nc, rows_in, cols_in, d_in, t_ref, *refs):
    x_refs, out_refs, refs = refs[:nc], refs[nc : nc + nr], refs[nc + nr :]
    rows, cols, d_ref, sems, xh, xl, acc = refs
    small = fetch((rows_in, cols_in, d_in), (rows, cols, d_ref), sems)
    fill(x_refs, xh, xl)
    acc[...] = jnp.zeros_like(acc)
    for copy in small:
        copy.wait()
    acc[0] = dot3((xh[0], xl[0]), split(d_ref[...]), NN)
    for slot in range(t_ref.shape[0]):
        j = row_slot(cols[slot], nr, -1)
        i = behind(rows[slot], nc)
        acc[j] += dot3((xh[i], xl[i]), split(t_ref[slot]), NN)
    for k in range(nr):
        out_refs[k][...] = acc[k]


def prepare_kernel(nr, nc, *refs):
    x_refs, r_refs, (th, tl, rh, rl) = refs[:nc], refs[nc : nc + nr], refs[nc + nr :]
    fill_turned(x_refs, th, tl)
    fill(r_refs, rh, rl)


def first_kernel(nr, nc, scale, places, rows_in, cols_in, live_in, t_ref, rh, rl, *refs):
    z_refs, refs = refs[: len(places)], refs[len(places) :]
    out_ref, rows, cols, live, sems, zh, zl = refs
    small = fetch((rows_in, cols_in, live_in), (rows, cols, live), sems)
    fill_turned(z_refs, zh, zl)
    for copy in small:
        copy.wait()
    for slot in range(t_ref.shape[0]):
        place = behind(rows[slot], nc)
        i = sum(jnp.where(place == p, k, 0) for k, p in enumerate(places))
        mine = functools.reduce(jnp.logical_or, [place == p for p in places])
        j = row_slot(cols[slot], nr, 1)
        gradient = dot3((zh[i], zl[i]), (rh[j], rl[j]), NN)
        step = jnp.where(jnp.logical_and(live[slot] > 0, mine), STEP_SIZE * scale, 0.0)
        out_ref[slot] = t_ref[slot] - step * gradient


def second_kernel(nr, nc, scale, places, rows_in, cols_in, live_in, d_in, v_ref, th, tl, *refs):
    z_refs, refs = refs[:nr], refs[nr:]
    out_ref, made, dout_ref, rows, cols, live, d_ref, sems, zh, zl, out_sems = refs
    small = fetch((rows_in, cols_in, live_in, d_in), (rows, cols, live, d_ref), sems)
    fill(z_refs, zh, zl)
    for copy in small:
        copy.wait()
    gradient = dot3((th[0], tl[0]), (zh[0], zl[0]), NN)
    gradient = (gradient + gradient.T) * scale
    tile = d_ref[...]
    row = lax.broadcasted_iota(jnp.int32, tile.shape, 0)
    on_diagonal = row == lax.broadcasted_iota(jnp.int32, tile.shape, 1)
    gradient = gradient - jnp.where(on_diagonal, 1.0 / jnp.where(on_diagonal, tile, 1.0), 0.0)
    value = tile - STEP_SIZE * gradient
    dout_ref[...] = jnp.where(on_diagonal, value, shrink(value, STEP_SIZE * PENALTY))
    copies, mine = [], []
    for slot in range(v_ref.shape[0]):
        j = row_slot(cols[slot], nr, 1)
        i = behind(rows[slot], nc)
        mine.append(functools.reduce(jnp.logical_or, [i == p for p in places]))
        copies.append(pltpu.make_async_copy(made.at[slot], out_ref.at[0, 0, slot], out_sems.at[slot]))
        gradient = dot3((th[i], tl[i]), (zh[j], zl[j]), NN)
        value = v_ref[slot] - jnp.where(live[slot] > 0, STEP_SIZE * scale, 0.0) * gradient
        whole = jnp.logical_and(live[slot] > 0, mine[slot])
        made[slot] = jnp.where(whole, shrink(value, STEP_SIZE * PENALTY), value)
    for slot in range(v_ref.shape[0]):
        pl.when(mine[slot])(copies[slot].start)
    for slot in range(v_ref.shape[0]):
        pl.when(mine[slot])(copies[slot].wait)


def late_kernel(nr, nc, scale, places, rows_in, cols_in, live_in, v_ref, rh, rl, *refs):
    z_refs, refs = refs[: len(places)], refs[len(places) :]
    _, out_ref, rows, cols, live, sems, zh, zl, made, out_sems = refs
    small = fetch((rows_in, cols_in, live_in), (rows, cols, live), sems)
    fill_turned(z_refs, zh, zl)
    for copy in small:
        copy.wait()
    mine, copies = [], []
    for slot in range(v_ref.shape[0]):
        place = behind(rows[slot], nc)
        i = sum(jnp.where(place == p, k, 0) for k, p in enumerate(places))
        mine.append(functools.reduce(jnp.logical_or, [place == p for p in places]))
        copies.append(pltpu.make_async_copy(made.at[slot], out_ref.at[0, 0, slot], out_sems.at[slot]))

        @pl.when(mine[slot])
        def _():
            j = row_slot(cols[slot], nr, 1)
            gradient = dot3((zh[i], zl[i]), (rh[j], rl[j]), NN)
            value = v_ref[slot]
            new = shrink(value - (STEP_SIZE * scale) * gradient, STEP_SIZE * PENALTY)
            made[slot] = jnp.where(live[slot] > 0, new, value)
            copies[slot].start()

    for slot in range(v_ref.shape[0]):
        pl.when(mine[slot])(copies[slot].wait)


def per_device(samples, omega_tiles, omega_diag, tile_rows, tile_cols, tile_active):
    nr = lax.axis_size("row")
    nc = lax.axis_size("col")
    count, side = samples.shape
    slots = omega_tiles.shape[2]
    scale = 1.0 / (2.0 * count)
    even_core = lax.axis_index("row") % 2 == 0

    ring = list(range(0, nc, 2)) + list(range(1, nc, 2))[::-1]
    right = [(ring[k], ring[(k + 1) % nc]) for k in range(nc)]
    left = [(b, a) for a, b in right]
    chip = [(k, (k + 2) % nr) for k in range(nr)]
    core = [(k, k ^ 1) for k in range(nr)]
    both = [
        (r * nc + a, r * nc + b) for r in range(nr) for a, b in (right if r % 2 == 0 else left)
    ]
    far = nc // 2
    go = lax.ppermute

    def ring_gather(own, beside):
        found = [own] + [None] * (nc - 1)
        for d in range(1, far + 1):
            one, two = found[d - 1], found[(nc - d + 1) % nc]
            if d in beside:
                one, two, _ = lax.optimization_barrier((one, two, beside[d](found)))
            if d < far:
                found[d] = go(one, "col", right)
                found[nc - d] = go(two, "col", left)
            else:
                found[far] = go(jnp.where(even_core, one, two), ("row", "col"), both)
        return found

    def ring_sum(parts):
        first = go(parts[far], ("row", "col"), both)
        one = jnp.where(even_core, parts[far - 1] + first, parts[far - 1])
        two = jnp.where(even_core, parts[far + 1], parts[far + 1] + first)
        for d in range(far - 1, 0, -1):
            one = go(one, "col", right)
            two = go(two, "col", left)
            if d > 1:
                one = parts[d - 1] + one
                two = parts[nc - d + 1] + two
        return parts[0], one, two

    def row_gather(own):
        found = [own]
        for _ in range(nr // 2 - 1):
            found.append(go(found[-1], "row", chip))
        return [a for b in found for a in (b, go(b, "row", core))]

    def row_sum(parts):
        sums = [parts[2 * k] + go(parts[2 * k + 1], "row", core) for k in range(nr // 2)]
        total = None
        for k in range(nr // 2 - 1, 0, -1):
            total = go(sums[k] if total is None else sums[k] + total, "row", chip)
        return (sums[0],) if total is None else (sums[0], total)

    whole = pl.BlockSpec(memory_space=pltpu.VMEM)
    in_place = pl.BlockSpec(memory_space=pltpu.HBM)

    def call(body, n_hbm, n_vmem, out_specs, out_shape, scratch, megabytes, aliases=None):
        return pl.pallas_call(
            body,
            in_specs=[in_place] * n_hbm + [whole] * n_vmem + [in_place] * len(aliases or {}),
            out_specs=out_specs,
            out_shape=out_shape,
            scratch_shapes=scratch,
            input_output_aliases=aliases or {},
            compiler_params=pltpu.CompilerParams(vmem_limit_bytes=megabytes * 1024 * 1024),
            cost_estimate=pl.CostEstimate(
                flops=6 * slots * count * side * side, bytes_accessed=COST_BYTES, transcendentals=0
            ),
        )

    def ids(n):
        return [pltpu.SMEM((slots,), jnp.int32)] * n

    def sems(n):
        return pltpu.SemaphoreType.DMA((n,))

    def panel(n):
        return [pltpu.VMEM((n, count, side), BF16)] * 2

    def panel_t(n):
        return [pltpu.VMEM((n, side, count), BF16)] * 2

    block = jax.ShapeDtypeStruct((count, side), F32)
    tile = jax.ShapeDtypeStruct((side, side), F32)
    tiles = jax.ShapeDtypeStruct((slots, side, side), F32)
    turned = jax.ShapeDtypeStruct((nc, side, count), BF16)
    straight = jax.ShapeDtypeStruct((nr, count, side), BF16)

    in_hbm = functools.partial(pltpu.with_memory_space_constraint, memory_space=pltpu.HBM)
    omega_tiles_raw = omega_tiles
    tile_rows, tile_cols, tile_active, omega_tiles, omega_diag = map(
        in_hbm, (tile_rows, tile_cols, tile_active, omega_tiles, omega_diag)
    )
    near = ()
    x_row, w = [], []

    def mirror(found):
        source = samples
        x_row.extend(row_gather(source))
        made_w = call(
            functools.partial(w_kernel, nr, nc, near),
            4,
            nr - 1,
            [whole if k in near else in_place for k in range(nc)],
            [block if k in near else pltpu.HBM((count, side), F32) for k in range(nc)],
            ids(2) + [pltpu.VMEM((count, side), F32), pltpu.VMEM((slots, side, side), F32), sems(3), sems(slots // GROUP), sems(nc)] + panel(nr) + [pltpu.VMEM((nc, count, side), F32)],
            10 + nc,
        )(tile_rows, tile_cols, in_hbm(samples), omega_tiles, *x_row[1:])
        w.extend(made_w)
        return w[0]

    x_col = ring_gather(samples, {far: mirror})
    held = omega_tiles_raw[0, 0]
    w_own = ring_sum(w)
    y = call(
        functools.partial(y_kernel, nr, nc),
        3,
        1 + nc,
        [whole] * nr,
        [block] * nr,
        ids(2) + [pltpu.VMEM((side, side), F32), sems(3)] + panel(nc) + [pltpu.VMEM((nr, count, side), F32)],
        10 + nc,
    )(tile_rows, tile_cols, omega_diag, held, *x_col)
    z = sum(row_sum(y)[::-1] + w_own)
    th, tl, rh, rl = call(
        functools.partial(prepare_kernel, nr, nc),
        0,
        nc + nr,
        [whole] * 4,
        [turned] * 2 + [straight] * 2,
        [],
        8,
    )(*x_col, *x_row)
    z, th, tl, rh, rl = lax.optimization_barrier((z, th, tl, rh, rl))
    made = []
    near_places, late_places, far_places = [0, 1, nc - 1], [p for d in range(2, far) for p in (d, nc - d)], [far]

    def first(found):
        made.append(
            call(
                functools.partial(first_kernel, nr, nc, scale, near_places),
                3,
                3 + len(near_places),
                whole,
                tiles,
                ids(3) + [sems(3)] + panel_t(len(near_places)),
                10 + nc,
            )(tile_rows, tile_cols, tile_active, held, rh, rl, *[found[p] for p in near_places])
        )
        return made[0]

    def second(found):
        z_row = row_gather(z)
        made.extend(
            call(
                functools.partial(second_kernel, nr, nc, scale, near_places),
                4,
                3 + nr,
                [in_place, whole, whole],
                [jax.ShapeDtypeStruct(omega_tiles.shape, F32), tiles, tile],
                ids(3) + [pltpu.VMEM((side, side), F32), sems(4)] + panel(nr) + [sems(slots)],
                10 + nc,
            )(tile_rows, tile_cols, tile_active, omega_diag, made[0], th, tl, *z_row)
        )
        return made[2]

    z_col = ring_gather(z, {far - 1: first, far: second})
    _, new_tiles, partial, new_diag = made
    for places in (late_places, far_places):
        new_tiles = call(
            functools.partial(late_kernel, nr, nc, scale, places),
            3,
            3 + len(places),
            in_place,
            jax.ShapeDtypeStruct(omega_tiles.shape, F32),
            ids(3)
            + [sems(3)]
            + panel_t(len(places))
            + [pltpu.VMEM((slots, side, side), F32), sems(slots)],
            10 + nc,
            {6 + len(places): 0},
        )(tile_rows, tile_cols, tile_active, partial, rh, rl, *[z_col[p] for p in places], new_tiles)
    return new_tiles, new_diag


def solution(mesh):
    in_specs = (
        P(None, ("row", "col")),
        P("row", "col", None, None, None),
        P(("row", "col"), None),
        P("row", "col", None),
        P("row", "col", None),
        P("row", "col", None),
    )
    out_specs = (P("row", "col", None, None, None), P(("row", "col"), None))
    return jax.shard_map(
        per_device, mesh=mesh, in_specs=in_specs, out_specs=out_specs, check_vma=False
    )
```

```python
import functools

import jax
import jax.numpy as jnp
from jax import lax
from jax.experimental import pallas as pl
from jax.experimental.pallas import tpu as pltpu
from jax.sharding import PartitionSpec as P

STEP_SIZE = 0.05
PENALTY = 4.0
F32 = jnp.float32
BF16 = jnp.bfloat16
COST_BYTES = 20_000_000
GROUP = 5
NN = (((1,), (0,)), ((), ()))
NT = (((1,), (1,)), ((), ()))


def split(values):
    high = values.astype(BF16)
    return high, (values - high.astype(F32)).astype(BF16)


def dot3(left, right, dims):
    (lh, ll), (rh, rl) = left, right
    mul = functools.partial(lax.dot_general, dimension_numbers=dims, preferred_element_type=F32)
    return mul(lh, rh) + (mul(ll, rh) + mul(lh, rl))


def shrink(values, limit):
    return jnp.maximum(values - limit, 0.0) + jnp.minimum(values + limit, 0.0)


def wrapped(index, count):
    return jnp.where(index < 0, index + count, index)


def ring_place(index, count):
    return jnp.where(index & 1 == 0, index >> 1, count - 1 - (index >> 1))


def behind(index, count):
    return wrapped(ring_place(lax.axis_index("col"), count) - ring_place(index, count), count)


def ahead(index, count):
    return wrapped(ring_place(index, count) - ring_place(lax.axis_index("col"), count), count)


def row_slot(index, count, sign):
    me = lax.axis_index("row")
    return 2 * wrapped(sign * ((me >> 1) - (index >> 1)), count // 2) + ((me + index) & 1)


def fill(refs, high, low):
    for k, ref in enumerate(refs):
        high[k], low[k] = split(ref[...])


def fill_turned(refs, high, low):
    for k, ref in enumerate(refs):
        high[k], low[k] = split(ref[...].T)


def fetch(sources, targets, sems):
    copies = [
        pltpu.make_async_copy(a.at[0, 0] if len(a.shape) == 3 else a, b, sems.at[k])
        for k, (a, b) in enumerate(zip(sources, targets))
    ]
    for copy in copies:
        copy.start()
    return copies


def w_kernel(nr, nc, near, rows_in, cols_in, own_in, t_in, *refs):
    x_refs, out_refs, refs = refs[: nr - 1], refs[nr - 1 : nr - 1 + nc], refs[nr - 1 + nc :]
    rows, cols, own, t_ref, sems, t_sems, out_sems, xh, xl, acc = refs
    small = fetch((own_in, rows_in, cols_in), (own, rows, cols), sems)
    groups = []
    for k in range(t_ref.shape[0] // GROUP):
        at = pl.ds(k * GROUP, GROUP)
        groups.append(pltpu.make_async_copy(t_in.at[0, 0, at], t_ref.at[at], t_sems.at[k]))
        groups[-1].start()
    for k, ref in enumerate(x_refs):
        xh[k + 1], xl[k + 1] = split(ref[...])
    acc[...] = jnp.zeros_like(acc)
    for copy in small:
        copy.wait()
    xh[0], xl[0] = split(own[...])
    for slot in range(t_ref.shape[0]):
        if slot % GROUP == 0:
            groups[slot // GROUP].wait()
        j = row_slot(cols[slot], nr, 1)
        i = ahead(rows[slot], nc)
        acc[i] += dot3((xh[j], xl[j]), split(t_ref[slot]), NT)
    copies = []
    for k in range(nc):
        if k in near:
            out_refs[k][...] = acc[k]
        else:
            copies.append(pltpu.make_async_copy(acc.at[k], out_refs[k], out_sems.at[k]))
            copies[-1].start()
    for copy in copies:
        copy.wait()


def y_kernel(nr, nc, rows_in, cols_in, d_in, t_ref, *refs):
    x_refs, out_refs, refs = refs[:nc], refs[nc : nc + nr], refs[nc + nr :]
    rows, cols, d_ref, sems, xh, xl, acc = refs
    small = fetch((rows_in, cols_in, d_in), (rows, cols, d_ref), sems)
    fill(x_refs, xh, xl)
    acc[...] = jnp.zeros_like(acc)
    for copy in small:
        copy.wait()
    acc[0] = dot3((xh[0], xl[0]), split(d_ref[...]), NN)
    for slot in range(t_ref.shape[0]):
        j = row_slot(cols[slot], nr, -1)
        i = behind(rows[slot], nc)
        acc[j] += dot3((xh[i], xl[i]), split(t_ref[slot]), NN)
    for k in range(nr):
        out_refs[k][...] = acc[k]


def prepare_kernel(nr, nc, *refs):
    x_refs, r_refs, (th, tl, rh, rl) = refs[:nc], refs[nc : nc + nr], refs[nc + nr :]
    fill_turned(x_refs, th, tl)
    fill(r_refs, rh, rl)


def first_kernel(nr, nc, scale, places, rows_in, cols_in, live_in, t_ref, rh, rl, *refs):
    z_refs, refs = refs[: len(places)], refs[len(places) :]
    out_ref, rows, cols, live, sems, zh, zl = refs
    small = fetch((rows_in, cols_in, live_in), (rows, cols, live), sems)
    fill_turned(z_refs, zh, zl)
    for copy in small:
        copy.wait()
    for slot in range(t_ref.shape[0]):
        place = behind(rows[slot], nc)
        i = sum(jnp.where(place == p, k, 0) for k, p in enumerate(places))
        mine = functools.reduce(jnp.logical_or, [place == p for p in places])
        j = row_slot(cols[slot], nr, 1)
        gradient = dot3((zh[i], zl[i]), (rh[j], rl[j]), NN)
        step = jnp.where(jnp.logical_and(live[slot] > 0, mine), STEP_SIZE * scale, 0.0)
        out_ref[slot] = t_ref[slot] - step * gradient


def second_kernel(nr, nc, scale, places, rows_in, cols_in, live_in, d_in, v_ref, th, tl, *refs):
    z_refs, refs = refs[:nr], refs[nr:]
    out_ref, made, dout_ref, rows, cols, live, d_ref, sems, zh, zl, out_sems = refs
    small = fetch((rows_in, cols_in, live_in, d_in), (rows, cols, live, d_ref), sems)
    fill(z_refs, zh, zl)
    for copy in small:
        copy.wait()
    gradient = dot3((th[0], tl[0]), (zh[0], zl[0]), NN)
    gradient = (gradient + gradient.T) * scale
    tile = d_ref[...]
    row = lax.broadcasted_iota(jnp.int32, tile.shape, 0)
    on_diagonal = row == lax.broadcasted_iota(jnp.int32, tile.shape, 1)
    gradient = gradient - jnp.where(on_diagonal, 1.0 / jnp.where(on_diagonal, tile, 1.0), 0.0)
    value = tile - STEP_SIZE * gradient
    dout_ref[...] = jnp.where(on_diagonal, value, shrink(value, STEP_SIZE * PENALTY))
    copies, mine = [], []
    for slot in range(v_ref.shape[0]):
        j = row_slot(cols[slot], nr, 1)
        i = behind(rows[slot], nc)
        mine.append(functools.reduce(jnp.logical_or, [i == p for p in places]))
        copies.append(pltpu.make_async_copy(made.at[slot], out_ref.at[0, 0, slot], out_sems.at[slot]))
        gradient = dot3((th[i], tl[i]), (zh[j], zl[j]), NN)
        value = v_ref[slot] - jnp.where(live[slot] > 0, STEP_SIZE * scale, 0.0) * gradient
        whole = jnp.logical_and(live[slot] > 0, mine[slot])
        made[slot] = jnp.where(whole, shrink(value, STEP_SIZE * PENALTY), value)
    for slot in range(v_ref.shape[0]):
        pl.when(mine[slot])(copies[slot].start)
    for slot in range(v_ref.shape[0]):
        pl.when(mine[slot])(copies[slot].wait)


def late_kernel(nr, nc, scale, places, parts, rows_in, cols_in, live_in, v_ref, rh, rl, *refs):
    z_refs, refs = refs[: parts * len(places)], refs[parts * len(places) :]
    _, out_ref, rows, cols, live, sems, zh, zl, made, out_sems = refs
    small = fetch((rows_in, cols_in, live_in), (rows, cols, live), sems)
    for k in range(len(places)):
        block = jnp.concatenate([ref[...] for ref in z_refs[parts * k : parts * (k + 1)]], axis=0)
        zh[k], zl[k] = split(block.T)
    for copy in small:
        copy.wait()
    mine, copies = [], []
    for slot in range(v_ref.shape[0]):
        place = behind(rows[slot], nc)
        i = sum(jnp.where(place == p, k, 0) for k, p in enumerate(places))
        mine.append(functools.reduce(jnp.logical_or, [place == p for p in places]))
        copies.append(pltpu.make_async_copy(made.at[slot], out_ref.at[0, 0, slot], out_sems.at[slot]))

        @pl.when(mine[slot])
        def _():
            j = row_slot(cols[slot], nr, 1)
            gradient = dot3((zh[i], zl[i]), (rh[j], rl[j]), NN)
            value = v_ref[slot]
            new = shrink(value - (STEP_SIZE * scale) * gradient, STEP_SIZE * PENALTY)
            made[slot] = jnp.where(live[slot] > 0, new, value)
            copies[slot].start()

    for slot in range(v_ref.shape[0]):
        pl.when(mine[slot])(copies[slot].wait)


def per_device(samples, omega_tiles, omega_diag, tile_rows, tile_cols, tile_active):
    nr = lax.axis_size("row")
    nc = lax.axis_size("col")
    count, side = samples.shape
    slots = omega_tiles.shape[2]
    scale = 1.0 / (2.0 * count)
    even_core = lax.axis_index("row") % 2 == 0

    ring = list(range(0, nc, 2)) + list(range(1, nc, 2))[::-1]
    right = [(ring[k], ring[(k + 1) % nc]) for k in range(nc)]
    left = [(b, a) for a, b in right]
    chip = [(k, (k + 2) % nr) for k in range(nr)]
    core = [(k, k ^ 1) for k in range(nr)]
    both = [
        (r * nc + a, r * nc + b) for r in range(nr) for a, b in (right if r % 2 == 0 else left)
    ]
    far = nc // 2
    go = lax.ppermute

    def ring_gather(own, beside, cut=False):
        found = [own] + [None] * (nc - 1)
        for d in range(1, far + 1):
            one, two = found[d - 1], found[(nc - d + 1) % nc]
            if d in beside:
                one, two, _ = lax.optimization_barrier((one, two, beside[d](found)))
            if d == far and cut:
                half = own.shape[0] // 2
                found[far] = (go(one[:half], "col", right), go(two[half:], "col", left))
            elif d < far:
                found[d] = go(one, "col", right)
                found[nc - d] = go(two, "col", left)
            else:
                found[far] = go(jnp.where(even_core, one, two), ("row", "col"), both)
        return found

    def ring_sum(parts):
        first = go(parts[far], ("row", "col"), both)
        one = jnp.where(even_core, parts[far - 1] + first, parts[far - 1])
        two = jnp.where(even_core, parts[far + 1], parts[far + 1] + first)
        for d in range(far - 1, 0, -1):
            one = go(one, "col", right)
            two = go(two, "col", left)
            if d > 1:
                one = parts[d - 1] + one
                two = parts[nc - d + 1] + two
        return parts[0], one, two

    def row_gather(own):
        found = [own]
        for _ in range(nr // 2 - 1):
            found.append(go(found[-1], "row", chip))
        return [a for b in found for a in (b, go(b, "row", core))]

    def row_sum(parts):
        sums = [parts[2 * k] + go(parts[2 * k + 1], "row", core) for k in range(nr // 2)]
        total = None
        for k in range(nr // 2 - 1, 0, -1):
            total = go(sums[k] if total is None else sums[k] + total, "row", chip)
        return (sums[0],) if total is None else (sums[0], total)

    whole = pl.BlockSpec(memory_space=pltpu.VMEM)
    in_place = pl.BlockSpec(memory_space=pltpu.HBM)

    def call(body, n_hbm, n_vmem, out_specs, out_shape, scratch, megabytes, aliases=None):
        return pl.pallas_call(
            body,
            in_specs=[in_place] * n_hbm + [whole] * n_vmem + [in_place] * len(aliases or {}),
            out_specs=out_specs,
            out_shape=out_shape,
            scratch_shapes=scratch,
            input_output_aliases=aliases or {},
            compiler_params=pltpu.CompilerParams(vmem_limit_bytes=megabytes * 1024 * 1024),
            cost_estimate=pl.CostEstimate(
                flops=6 * slots * count * side * side, bytes_accessed=COST_BYTES, transcendentals=0
            ),
        )

    def ids(n):
        return [pltpu.SMEM((slots,), jnp.int32)] * n

    def sems(n):
        return pltpu.SemaphoreType.DMA((n,))

    def panel(n):
        return [pltpu.VMEM((n, count, side), BF16)] * 2

    def panel_t(n):
        return [pltpu.VMEM((n, side, count), BF16)] * 2

    block = jax.ShapeDtypeStruct((count, side), F32)
    tile = jax.ShapeDtypeStruct((side, side), F32)
    tiles = jax.ShapeDtypeStruct((slots, side, side), F32)
    turned = jax.ShapeDtypeStruct((nc, side, count), BF16)
    straight = jax.ShapeDtypeStruct((nr, count, side), BF16)

    in_hbm = functools.partial(pltpu.with_memory_space_constraint, memory_space=pltpu.HBM)
    omega_tiles_raw = omega_tiles
    tile_rows, tile_cols, tile_active, omega_tiles, omega_diag = map(
        in_hbm, (tile_rows, tile_cols, tile_active, omega_tiles, omega_diag)
    )
    near = ()
    x_row, w = [], []

    def mirror(found):
        source = samples
        x_row.extend(row_gather(source))
        made_w = call(
            functools.partial(w_kernel, nr, nc, near),
            4,
            nr - 1,
            [whole if k in near else in_place for k in range(nc)],
            [block if k in near else pltpu.HBM((count, side), F32) for k in range(nc)],
            ids(2) + [pltpu.VMEM((count, side), F32), pltpu.VMEM((slots, side, side), F32), sems(3), sems(slots // GROUP), sems(nc)] + panel(nr) + [pltpu.VMEM((nc, count, side), F32)],
            10 + nc,
        )(tile_rows, tile_cols, in_hbm(samples), omega_tiles, *x_row[1:])
        w.extend(made_w)
        return w[0]

    x_col = ring_gather(samples, {far: mirror})
    held = omega_tiles_raw[0, 0]
    w_own = ring_sum(w)
    y = call(
        functools.partial(y_kernel, nr, nc),
        3,
        1 + nc,
        [whole] * nr,
        [block] * nr,
        ids(2) + [pltpu.VMEM((side, side), F32), sems(3)] + panel(nc) + [pltpu.VMEM((nr, count, side), F32)],
        10 + nc,
    )(tile_rows, tile_cols, omega_diag, held, *x_col)
    z = sum(row_sum(y)[::-1] + w_own)
    th, tl, rh, rl = call(
        functools.partial(prepare_kernel, nr, nc),
        0,
        nc + nr,
        [whole] * 4,
        [turned] * 2 + [straight] * 2,
        [],
        8,
    )(*x_col, *x_row)
    z, th, tl, rh, rl = lax.optimization_barrier((z, th, tl, rh, rl))
    made = []
    near_places, late_places, far_places = [0, 1, nc - 1], [p for d in range(2, far) for p in (d, nc - d)], [far]

    def first(found):
        made.append(
            call(
                functools.partial(first_kernel, nr, nc, scale, near_places),
                3,
                3 + len(near_places),
                whole,
                tiles,
                ids(3) + [sems(3)] + panel_t(len(near_places)),
                10 + nc,
            )(tile_rows, tile_cols, tile_active, held, rh, rl, *[found[p] for p in near_places])
        )
        return made[0]

    def second(found):
        z_row = row_gather(z)
        made.extend(
            call(
                functools.partial(second_kernel, nr, nc, scale, near_places),
                4,
                3 + nr,
                [in_place, whole, whole],
                [jax.ShapeDtypeStruct(omega_tiles.shape, F32), tiles, tile],
                ids(3) + [pltpu.VMEM((side, side), F32), sems(4)] + panel(nr) + [sems(slots)],
                10 + nc,
            )(tile_rows, tile_cols, tile_active, omega_diag, made[0], th, tl, *z_row)
        )
        return made[2]

    z_col = ring_gather(z, {far - 1: first, far: second}, True)
    _, new_tiles, partial, new_diag = made
    for places in (late_places, far_places):
        came = [a for p in places for a in (z_col[p] if isinstance(z_col[p], tuple) else (z_col[p],))]
        new_tiles = call(
            functools.partial(late_kernel, nr, nc, scale, places, len(came) // len(places)),
            3,
            3 + len(came),
            in_place,
            jax.ShapeDtypeStruct(omega_tiles.shape, F32),
            ids(3)
            + [sems(3)]
            + panel_t(len(places))
            + [pltpu.VMEM((slots, side, side), F32), sems(slots)],
            10 + nc,
            {6 + len(came): 0},
        )(tile_rows, tile_cols, tile_active, partial, rh, rl, *came, new_tiles)
    return new_tiles, new_diag


def solution(mesh):
    in_specs = (
        P(None, ("row", "col")),
        P("row", "col", None, None, None),
        P(("row", "col"), None),
        P("row", "col", None),
        P("row", "col", None),
        P("row", "col", None),
    )
    out_specs = (P("row", "col", None, None, None), P(("row", "col"), None))
    return jax.shard_map(
        per_device, mesh=mesh, in_specs=in_specs, out_specs=out_specs, check_vma=False
    )
```
